512 devices in a mesh: gx: 16 (over z), gy: 8 (over x, core), gz: 4 (over y).
Axes of the slice: x: 4, y: 4, z: 16, core: 2. Of those that a mesh axis runs over, the one named last changes fastest.
Arguments:
- fluid_adjoint: float32 [128, 128, 512], P('gx', 'gy', 'gz'), may hold values from -6 to 6
- fluid_source: float32 [128, 128, 512], P('gx', 'gy', 'gz'), may hold values from -6 to 6
- inverse_x: float32 [128, 8], P('gx')
- inverse_y: float32 [128, 16], P('gy')
- inverse_z: float32 [512, 128], P('gz')
- face_cells: int32 [262144, 4], P(('gx', 'gy', 'gz')), may hold values from 0 to 16383
- face_weight: float32 [262144, 4], P(('gx', 'gy', 'gz')), may hold values from 0.1 to 1
- face_owner: int32 [262144, 1], P(('gx', 'gy', 'gz')), may hold values from 0 to 31; in each aligned block of 512 rows (0 to 511, 512 to 1023, ...) at most 40 rows name the same one
- face_solid: int32 [262144], P(('gx', 'gy', 'gz')), may hold values from 0 to 511
- solid_inverse: float32 [262144, 512], P(('gx', 'gy', 'gz'))
- solid_source: float32 [262144], P(('gx', 'gy', 'gz')), may hold values from -6 to 6
Outputs:
- fluid_result: float32 [128, 128, 512], P('gx', 'gy', 'gz')
- solid_adjoint: float32 [262144], P(('gx', 'gy', 'gz'))
The draws below stay inside these ranges and needn't reach their ends.
Inputs may be any that keep to these rules, and one draw needn't show every extreme that they name: `face_owner`: within the faces of one fluid device, no owner is named by more than 40 faces, a bound that some block reaches.
All inputs are finite; a program needn't handle non-finite values.
Results may differ from the reference program's by a relative error of at most 0.0001.
Values sent between devices are 32-bit elements; how exact they have to be, the bound alone decides.
No kernel may reach another device: no remote copies, remote signals or barrier semaphores. Data moves between devices by JAX's collectives and lax.ppermute only.
A program may use at most 64 MiB of HBM per device.

```python
import math
import jax
import jax.numpy as jnp
import numpy as np
from jax import lax

CX = 8
CY = 16
CZ = 128
SWEEPS = 8
FACE_DEV = 512
SOL_DEV = 512
NX = 128
NY = 128
NZ = 512
NF = 262144
NS = 262144
CAP = 40
N_GX = 16
N_GY = 8
N_GZ = 4


def diagonal_part(key, blocks, extent):
    row_pos = jnp.arange(blocks * extent, dtype=jnp.int32)[:, None] % extent
    col_pos = jnp.arange(extent, dtype=jnp.int32)[None, :]
    scales = jax.random.uniform(key, (blocks * extent, 1), jnp.float32, 0.8, 1.2)
    return jnp.where(row_pos == col_pos, scales, 0.0)


def draw_inverse_x(key, part):
    key = jax.random.fold_in(key, 11)
    first, second = jax.random.split(key)
    noise = jax.random.normal(second, (NX, CX), jnp.float32) * 0.25
    return diagonal_part(first, NX // CX, CX) + noise / math.sqrt(CX)


def draw_inverse_y(key, part):
    key = jax.random.fold_in(key, 12)
    first, second = jax.random.split(key)
    noise = jax.random.normal(second, (NY, CY), jnp.float32) * 0.25
    return diagonal_part(first, NY // CY, CY) + noise / math.sqrt(CY)


def draw_inverse_z(key, part):
    key = jax.random.fold_in(key, 13)
    first, second = jax.random.split(key)
    noise = jax.random.normal(second, (NZ, CZ), jnp.float32) * 0.25
    return diagonal_part(first, NZ // CZ, CZ) + noise / math.sqrt(CZ)


def draw_solid_inverse(key, part):
    key = jax.random.fold_in(key, 14)
    first, second = jax.random.split(key)
    noise = jax.random.normal(second, (NS, SOL_DEV), jnp.float32) * 0.25
    return diagonal_part(first, NS // SOL_DEV, SOL_DEV) + noise / math.sqrt(SOL_DEV)


def with_ends(drawn, rng, smallest, largest):
    index_at = [jax.random.randint(jax.random.fold_in(rng, axis), (), 0, length) for axis, length in enumerate(drawn.shape)]
    longest = drawn.shape.index(max(drawn.shape))
    neighbour = index_at[:longest] + [(index_at[longest] + 1) % drawn.shape[longest]] + index_at[longest + 1:]
    return drawn.at[tuple(index_at)].set(smallest).at[tuple(neighbour)].set(largest)


def level_of(stream_key, shape, cuts, least, top_value):
    def one(position, blocks):
        draws = jax.random.uniform(jax.random.fold_in(jax.random.fold_in(stream_key, 6), position), (blocks,), jnp.float32, least / len(cuts), top_value / len(cuts))
        return jnp.repeat(jnp.exp(draws), shape[position] // blocks).reshape((-1,) + (1,) * (len(shape) - position - 1))

    gain = one(*cuts[0])
    for cut in cuts[1:]:
        gain = gain * one(*cut)
    return gain


def deal_out(stream_key, own, number, rows, count, top, reach, skew):
    sequence = jax.random.permutation(stream_key, count)
    heavy_load, common = load_shares(count, rows * top, reach, skew, True), load_shares(count, rows * top, reach, skew, False)
    places = jnp.arange(count)

    def named(sizes, rotation):
        used = int((sizes > 0).sum())
        fixed = max(1, used // 4)
        moved = fixed + (places - fixed + rotation * (used - fixed)) % max(1, count - fixed)
        return jnp.zeros((count,), jnp.int32).at[sequence[jnp.where(places < fixed, places, moved)]].set(jnp.asarray(sizes, jnp.int32))

    sizes = jnp.where(number % 4 == 0, named(heavy_load, number // 4), named(common, number - number // 4 - 1))
    mixed = jax.random.permutation(jax.random.fold_in(own, 3), count)
    giver, sink = mixed[0:count // 2 * 2:2], mixed[1:count // 2 * 2:2]
    slack = jnp.minimum(sizes[giver] - 1, reach - sizes[sink]) // 2
    slack = jnp.where((giver == sequence[0]) | (sink == sequence[0]) | (sizes[sink] == 0), 0, jnp.maximum(slack, 0))
    moved = jax.random.randint(jax.random.fold_in(own, 4), (count // 2,), 0, 1 << 20) % (slack + 1)
    sizes = sizes.at[giver].add(-moved).at[sink].add(moved)
    labels = jnp.searchsorted(jnp.cumsum(sizes), jnp.arange(rows * top), side="right").astype(jnp.int32)
    grid = labels.reshape(top, rows).T
    grid = grid[jax.random.permutation(jax.random.fold_in(own, 1), rows)]
    rotation = jax.random.randint(jax.random.fold_in(own, 2), (rows, 1), 0, top)
    return jnp.take_along_axis(grid, (jnp.arange(top)[None, :] + rotation) % top, axis=1)


def load_shares(count, total, most, lean, full):
    weights = [(1 << 20) // math.isqrt(standing ** lean) + 1 for standing in range(1, count + 1)]
    largest = most if full else min(most, max(-(-total // count), total * weights[0] // sum(weights)))
    least = 1 if total - largest >= count - 1 else 0
    holding, surplus = [largest] + [least] * (count - 1), total - largest - least * (count - 1)
    while surplus > 0:
        movable = [i for i in range(1, count) if holding[i] < largest] or [i for i in range(1, count) if holding[i] < most]
        mass, remaining = sum([weights[i] for i in movable]), surplus
        for i in movable:
            extra = min(most - holding[i], max(1, remaining * weights[i] // mass), surplus)
            holding[i] = holding[i] + extra
            surplus = surplus - extra
    return np.array(holding)


def normal_values(own_key, shape, width, limit, cuts=(), kind=jnp.bfloat16):
    factor_of = level_of(own_key, shape, cuts, -0.22, 0.18) if cuts else 1.0
    values = jax.random.normal(own_key, shape, jnp.float32) * width * factor_of
    return jnp.minimum(jnp.maximum(values, -limit), limit).astype(kind)


def setup_inputs(seed: int = 0) -> dict:
    key_list = jax.random.split(jax.random.key(seed), 12)
    fluid_adjoint = normal_values(key_list[0], (NX, NY, NZ), 1.0, 6.0, ((0, 16), (1, 8), (2, 4)), jnp.float32)
    fluid_source = normal_values(key_list[1], (NX, NY, NZ), 1.0, 6.0, ((0, 16), (1, 8), (2, 4)), jnp.float32)
    inverse_x = draw_inverse_x(jax.random.fold_in(key_list[11], 71), 0)
    inverse_y = draw_inverse_y(jax.random.fold_in(key_list[11], 71), 0)
    inverse_z = draw_inverse_z(jax.random.fold_in(key_list[11], 71), 0)
    face_cells = with_ends(jax.random.randint(key_list[5], (NF, 4), 0, CX * CY * CZ), jax.random.fold_in(key_list[5], 1), 0, (CX * CY * CZ) - 1).astype(jnp.int32)
    face_weight = jnp.clip(0.1 + 0.9 * jax.random.uniform(key_list[6], (NF, 4), jnp.float32) ** level_of(key_list[6], (NF, 4), ((0, 512),), -0.2, 0.2), 0.1, 1.0)
    face_owner_keys = jax.random.split(jax.random.fold_in(key_list[7], 1), NF // FACE_DEV)
    face_owner_turns = jax.random.permutation(jax.random.fold_in(key_list[7], 3), NF // FACE_DEV)
    face_owner = jax.vmap(lambda own, number: deal_out(jax.random.fold_in(key_list[7], 2), own, number, FACE_DEV, N_GY * N_GZ, 1, CAP, 2))(face_owner_keys, face_owner_turns).reshape((NF, 1))
    face_solid = with_ends(jax.random.randint(key_list[8], (NF,), 0, SOL_DEV), jax.random.fold_in(key_list[8], 1), 0, SOL_DEV - 1).astype(jnp.int32)
    solid_inverse = draw_solid_inverse(jax.random.fold_in(key_list[11], 71), 0)
    solid_source = normal_values(key_list[10], (NS,), 1.0, 6.0, ((0, 512),), jnp.float32)
    return {"fluid_adjoint": fluid_adjoint, "fluid_source": fluid_source, "inverse_x": inverse_x, "inverse_y": inverse_y, "inverse_z": inverse_z, "face_cells": face_cells, "face_weight": face_weight, "face_owner": face_owner, "face_solid": face_solid, "solid_inverse": solid_inverse, "solid_source": solid_source}


RELAX = 0.15
SPREAD = 0.06
COUPLE = 0.5


def stencil(extended, along, length):
    pieces = [lax.slice_in_dim(extended, offset, offset + length, axis=along) for offset in range(5)]
    return (16.0 * (pieces[1] + pieces[3]) - 30.0 * pieces[2] - pieces[0] - pieces[4]) / 12.0


def block_apply(matrix, operand, along, blocks, extent):
    shape = operand.shape
    mats = matrix.reshape(blocks, extent, extent)
    if along == 0:
        split = operand.reshape(blocks, extent, shape[1], shape[2])
        result = jnp.einsum("gjab,gji->giab", split, mats, precision=lax.Precision.HIGHEST)
    elif along == 1:
        split = operand.reshape(shape[0], blocks, extent, shape[2])
        result = jnp.einsum("agjb,gji->agib", split, mats, precision=lax.Precision.HIGHEST)
    else:
        split = operand.reshape(shape[0], shape[1], blocks, extent)
        result = jnp.einsum("abgj,gji->abgi", split, mats, precision=lax.Precision.HIGHEST)
    return result.reshape(shape)


def direction_term(matrix, adjoint, along, blocks, extent):
    padding = [(0, 0), (0, 0), (0, 0)]
    padding[along] = (2, 2)
    extended = jnp.pad(adjoint, padding)
    return block_apply(matrix, stencil(extended, along, adjoint.shape[along]), along, blocks, extent)


def reference(fluid_adjoint, fluid_source, inverse_x, inverse_y, inverse_z, face_cells, face_weight, face_owner, face_solid, solid_inverse, solid_source):
    adjoint = fluid_adjoint
    for sweep in range(SWEEPS):
        total = direction_term(inverse_x, adjoint, 0, N_GX, CX)
        total = total + direction_term(inverse_y, adjoint, 1, N_GY, CY)
        total = total + direction_term(inverse_z, adjoint, 2, N_GZ, CZ)
        adjoint = adjoint + RELAX * (fluid_source - adjoint) + SPREAD * total
    devices = N_GX * N_GY * N_GZ
    owners = N_GY * N_GZ
    block_cells = CX * CY * CZ
    blocked = fluid_adjoint.reshape(N_GX, CX, N_GY, CY, N_GZ, CZ).transpose(0, 2, 4, 1, 3, 5).reshape(devices, block_cells)
    device_of = (jnp.arange(NF, dtype=jnp.int32) // FACE_DEV).astype(jnp.int32)
    flux = jnp.sum(face_weight * blocked[device_of[:, None], face_cells], axis=1)
    owner_device = (device_of // owners) * owners + face_owner[:, 0]
    solid_index = (owner_device * SOL_DEV + face_solid).astype(jnp.int32)
    heat = solid_source + jnp.zeros((NS,), jnp.float32).at[solid_index].add(flux)
    mats = solid_inverse.reshape(devices, SOL_DEV, SOL_DEV)
    solid_adjoint = jnp.einsum("dj,dji->di", heat.reshape(devices, SOL_DEV), mats, precision=lax.Precision.HIGHEST).reshape(NS)
    face_temp = solid_adjoint[solid_index]
    flat_index = (device_of[:, None] * block_cells + face_cells).astype(jnp.int32)
    coupled = jnp.zeros((devices * block_cells,), jnp.float32).at[flat_index.reshape(-1)].add((face_weight * face_temp[:, None]).reshape(-1))
    coupled = coupled.reshape(N_GX, N_GY, N_GZ, CX, CY, CZ).transpose(0, 3, 1, 4, 2, 5).reshape(NX, NY, NZ)
    return adjoint + COUPLE * coupled, solid_adjoint
```

```python
import math
import jax
import jax.numpy as jnp
from jax import lax
from jax.experimental import pallas as pl
from jax.experimental.pallas import tpu as pltpu
from jax.sharding import PartitionSpec as P

SWEEPS = 8
RELAX = 0.15
SPREAD = 0.06
COUPLE = 0.5
SHIFT = 0.25

F32 = jnp.float32
BF16 = jnp.bfloat16
VMEM_LIMIT = 16 * 1024 * 1024
HI = lax.Precision.HIGHEST


def iota(shape, dim):
    return lax.broadcasted_iota(jnp.int32, shape, dim)


def dot(a, b, dims=((1,), (0,)), precision=HI):
    return lax.dot_general(a, b, (dims, ((), ())), precision=precision, preferred_element_type=F32)


def narrow_dot(a, b, dims=((1,), (0,))):
    return lax.dot_general(a, b, (dims, ((), ())), preferred_element_type=F32)


def split2(v):
    p1 = v.astype(BF16)
    return p1, (v - p1.astype(F32)).astype(BF16)


def split3(v):
    p1 = v.astype(BF16)
    rest = v - p1.astype(F32)
    p2 = rest.astype(BF16)
    p3 = (rest - p2.astype(F32)).astype(BF16)
    return p1, p2, p3


def hot_dot(values, hot, dims):
    parts = [narrow_dot(p, hot, dims) for p in split3(values)]
    return parts[0] + (parts[1] + parts[2])


def hot_rows(index_row, count):
    return iota((count, index_row.shape[1]), 0) == index_row


def ones_of(mask):
    return jnp.where(mask, 1.0, 0.0).astype(BF16)


def weights_of(far):
    return jnp.where(
        far == 0, -30.0 / 12.0, jnp.where(far == 1, 16.0 / 12.0, jnp.where(far == 2, -1.0 / 12.0, 0.0))
    )


VM = pl.BlockSpec(memory_space=pltpu.VMEM)
ANY = pl.BlockSpec(memory_space=pl.ANY)


def call(body, outs, *args, specs=None, scratch=(), limit=VMEM_LIMIT, flops=1000000, touched=100000):
    return pl.pallas_call(
        body,
        out_shape=outs,
        in_specs=[VM] * len(args) if specs is None else specs,
        out_specs=jax.tree.map(lambda _: VM, outs),
        scratch_shapes=list(scratch),
        compiler_params=pltpu.CompilerParams(vmem_limit_bytes=limit),
        cost_estimate=pl.CostEstimate(flops=flops, bytes_accessed=touched, transcendentals=0),
    )(*args)


def load_all(sem, pairs):
    copies = [pltpu.make_async_copy(src, dst, sem.at[n]) for n, (src, dst) in enumerate(pairs)]
    for c in copies:
        c.start()
    for c in copies:
        c.wait()


def wide_dot(a, b):
    high, low = split2(b)
    return narrow_dot(a[0], high) + (narrow_dot(a[0], low) + narrow_dot(a[1], high))


def put_split(ref, cols, value):
    high, low = split2(value)
    ref[0, :, cols] = high
    ref[1, :, cols] = low


def pack_body(table_hbm, source_hbm, inv_hbm, out_ref, table_ref, source_ref, inv_ref, sem):
    load_all(sem, [(table_hbm, table_ref), (source_hbm, source_ref), (inv_hbm, inv_ref)])
    inv = jnp.concatenate([inv_ref[r : r + 1, :] for r in range(8)] + [jnp.zeros((1, 64), F32)], axis=1)
    for y in range(16):
        out_ref[17 * y : 17 * y + 8, :] = table_ref[pl.ds(y, 8, stride=16), :]
        out_ref[17 * y + 8 : 17 * y + 16, :] = source_ref[pl.ds(y, 8, stride=16), :]
        out_ref[17 * y + 16 : 17 * y + 17, :] = inv


def lines_body(recv_ref, out_ref, token_ref, power):
    token_ref[...] = jnp.zeros((8, 128), F32)
    row, col = iota((128, 128), 0), iota((128, 128), 1)
    inv = recv_ref[pl.ds(16, 16, stride=17), :]
    rows = jnp.where((iota((128, 16), 0) >> 3) == iota((128, 16), 1), 1.0, 0.0).astype(BF16)
    first, second = split2(inv)
    wide = narrow_dot(rows, first) + narrow_dot(rows, second)
    wide = jnp.where((row & 7) == (col & 7), wide, 0.0)
    pick = ones_of((row < 64) & ((row >> 3) == (col & 7)))
    first, second = split2(wide)
    diag = narrow_dot(first, pick) + narrow_dot(second, pick)
    diag = jnp.where((row >> 3) == (col >> 3), diag, 0.0)
    far = jnp.abs(row - col)
    first, second = split2(diag)
    band = jnp.where(far == 0, -30.0, jnp.where(far == 1, 16.0, jnp.where(far == 2, -1.0, 0.0))).astype(BF16)
    op = (SPREAD / 12.0) * (narrow_dot(first, band) + narrow_dot(second, band)) + jnp.where(far == 0, SHIFT, 0.0)
    for f in range(2):
        power[:, 128 * f : 128 * f + 128] = jnp.concatenate(
            [recv_ref[17 * g + 8 * f : 17 * g + 8 * f + 8, :] for g in range(16)], axis=0
        )

    def store(k, value):
        power[:, 256 * k : 256 * k + value.shape[1]] = value

    both = wide_dot(split2(op), jnp.concatenate([op, power[:, 0:256]], axis=1))
    store(1, both[:, 128:])
    both = wide_dot(split2(both[:, 0:128]), jnp.concatenate([both[:, 0:128], power[:, 0:512]], axis=1))
    store(2, both[:, 128:])
    four = split2(both[:, 0:128])
    store(4, wide_dot(four, power[:, 0:1024]))
    store(8, wide_dot(four, power[:, 1024 : 1024 + 128]))
    for m in range(SWEEPS - 1):
        total = float(math.comb(SWEEPS, m)) * power[:, 256 * (SWEEPS - m) : 256 * (SWEEPS - m) + 128]
        for i in range(m, SWEEPS):
            total = total + RELAX * math.comb(i, m) * power[:, 256 * (i - m) + 128 : 256 * (i - m) + 256]
        for g in range(16):
            out_ref[56 * g + 8 * m : 56 * g + 8 * m + 8, :] = total[8 * g : 8 * g + 8]


def near_body(table_ref, low_ref, high_ref, source_hbm, inv_ref, out_ref, source_ref, sem):
    load_all(sem, [(source_hbm, source_ref)])
    layers = [low_ref[0:16, :], low_ref[16:32, :]]
    layers += [table_ref[16 * x : 16 * x + 16, :] for x in range(8)]
    layers += [high_ref[0:16, :], high_ref[16:32, :]]
    sums = [
        16.0 * (layers[x + 1] + layers[x + 3]) - 30.0 * layers[x + 2] - layers[x] - layers[x + 4] for x in range(8)
    ]
    for i in range(8):
        total = sums[0] * inv_ref[0, i]
        for r in range(1, 8):
            total = total + sums[r] * inv_ref[r, i]
        total = (SPREAD / 12.0) * total + SHIFT * layers[i + 2]
        rows = slice(16 * i, 16 * i + 16)
        out_ref[rows, :] = SWEEPS * total + RELAX * source_ref[rows, :]


def deal_body(recv_ref, table_ref, near_ref, heat_ref, rows_ref, after_one, after_two, out_ref, first_ref):
    for m in range(SWEEPS - 1):
        for y in range(16):
            rows = recv_ref[56 * y + 8 * m : 56 * y + 8 * m + 8, :]
            if m == 0:
                first_ref[pl.ds(y, 8, stride=16), :] = rows
            else:
                q, half = divmod(m - 1, 2)
                out_ref[pl.ds(40 * q + 16 * half + y, 8, stride=160), :] = rows
    for x in range(8):
        out_ref[160 * x + 120 : 160 * x + 136, :] = near_ref[16 * x : 16 * x + 16, :]
        out_ref[160 * x + 136 : 160 * x + 152, :] = table_ref[16 * x : 16 * x + 16, :]
    for h in range(4):
        out_ref[pl.ds(32 + h, 32, stride=40), :] = heat_ref[h * 32 : (h + 1) * 32, :]
    for o in range(32):
        out_ref[40 * o + 36 : 40 * o + 40, :] = rows_ref[0:4, :]


def send_body(table_ref, cells_ref, weight_ref, owner_ref, solid_ref, inv_y_ref, inv_z_in, after_ref, out_ref, rows_ref, inv_z_ref, low_ref, high_ref):
    gy = lax.axis_index("gy")
    gz = lax.axis_index("gz")
    inv_z_ref[...] = inv_z_in[...]
    low_ref[...] = table_ref[0:32, :]
    high_ref[...] = table_ref[96:128, :]
    table = table_ref[...]
    acc = None
    for k in range(4):
        cell = cells_ref[k : k + 1, :]
        hot = ones_of(hot_rows(cell >> 7, 128))
        spread = jnp.where(hot_rows(cell & 127, 128), weight_ref[k : k + 1, :], 0.0)
        term = hot_dot(table, hot, ((0,), (0,))) * spread
        acc = term if acc is None else acc + term
    flux = jnp.sum(acc, axis=0, keepdims=True)
    solid = solid_ref[...]
    owner = owner_ref[...]
    rank = (owner & 3) * 8 + (owner >> 2)
    hot_hi = ones_of(hot_rows((solid >> 7) * 32 + rank, 128))
    out_ref[...] = hot_dot(jnp.where(hot_rows(solid & 127, 128), flux, 0.0), hot_hi, ((1,), (1,))).T
    shift = iota((16, 128), 1) - gy * 16 - iota((16, 128), 0)
    own = SPREAD * dot(inv_y_ref[...], weights_of(jnp.abs(shift)), ((0,), (0,)))
    own = own + jnp.where(shift == 0, 1.0 - RELAX - SHIFT, 0.0)
    pick = jnp.where(iota((8, 16), 1) == iota((8, 16), 0) + gz * 4, 1.0, 0.0)
    rows_ref[...] = dot(pick, own)


def split_body(value_hbm, after_hbm, out_ref, value_ref, sem):
    load_all(sem, [(value_hbm, value_ref)])
    put_split(out_ref, slice(0, 512), value_ref[...])


def finish_body(recv_ref, first_ref, cells_ref, weight_ref, owner_ref, solid_ref, out_ref, stage):
    for o in range(32):
        owner = (o % 8) * 4 + o // 8
        stage[4 * owner : 4 * owner + 4, :] = recv_ref[20 * o + 16 : 20 * o + 20, :]
    solid = solid_ref[...]
    hot = ones_of(hot_rows(owner_ref[...] * 4 + (solid >> 7), 128))
    high, rest = split2(stage[...])
    picked = narrow_dot(high, hot, ((0,), (0,))) + narrow_dot(rest, hot, ((0,), (0,)))
    temp = COUPLE * jnp.sum(jnp.where(hot_rows(solid & 127, 128), picked, 0.0), axis=0, keepdims=True)
    hots, highs, rests = [], [], []
    for k in range(4):
        cell = cells_ref[k : k + 1, :]
        hots.append(ones_of(hot_rows(cell >> 7, 128)))
        high, rest = split2(jnp.where(hot_rows(cell & 127, 128), temp * weight_ref[k : k + 1, :], 0.0))
        highs.append(high)
        rests.append(rest)
    hot = jnp.concatenate(hots, axis=1)
    total = narrow_dot(hot, jnp.concatenate(highs, axis=1), ((1,), (1,)))
    total = total + narrow_dot(hot, jnp.concatenate(rests, axis=1), ((1,), (1,)))
    for i in range(8):
        parts = [recv_ref[20 * o : 20 * o + 16, :] for o in range(4 * i, 4 * i + 4)]
        part = (parts[0] + parts[1]) + (parts[2] + parts[3])
        rows = slice(16 * i, 16 * i + 16)
        out_ref[i] = part + first_ref[rows, :] + total[rows, :]


def prepare_body(own_ref, one_ref, two_ref, three_ref, op_z_ref, mats):
    gz = lax.axis_index("gz")
    for d, ref in enumerate((own_ref, one_ref, two_ref, three_ref)):
        mats[jnp.bitwise_xor(gz, d)] = ref[...]
    for k in range(4):
        far = jnp.abs(iota((512, 128), 0) - (iota((512, 128), 1) + 128 * k))
        put_split(op_z_ref, slice(128 * k, 128 * k + 128), SPREAD * dot(weights_of(far), mats[k]))


def planes_body(recv_ref, op_z_ref, source_ref, inverse_ref, out_ref, line_ref, low, acc, op_y):
    q = lax.rem(lax.axis_index("gy"), 4)
    for o in range(32):
        z, y = divmod(o, 8)
        low[16 * y : 16 * y + 16, 128 * z : 128 * (z + 1)] = recv_ref[o, 0:16]
        acc[16 * y : 16 * y + 16, 128 * z : 128 * (z + 1)] = recv_ref[o, 16:32]
        op_y[16 * y + 4 * z : 16 * y + 4 * z + 4, :] = recv_ref[o, 36:40]
    y_high, y_low = split2(op_y[...])
    y_both = jnp.concatenate([y_high, y_high], axis=1)

    def apply():
        high, rest = split2(acc[...])
        along_y = narrow_dot(y_both, jnp.concatenate([high, rest], axis=0)) + narrow_dot(y_low, high)
        along_z = narrow_dot(high, op_z_ref[0]) + (narrow_dot(high, op_z_ref[1]) + narrow_dot(rest, op_z_ref[0]))
        return along_y + along_z

    heat = jnp.sum(recv_ref[:, 32:40, :], axis=0)[0:4, :] + source_ref[...]
    high, rest = split2(jnp.concatenate([heat[h : h + 1, :] for h in range(4)], axis=1))
    both = jnp.concatenate([high.astype(F32), rest.astype(F32), jnp.zeros((6, 512), F32)], axis=0).astype(BF16)
    result = narrow_dot(both, inverse_ref[0])
    result = (result[0:1] + result[1:2]) + narrow_dot(both, inverse_ref[1])[0:1]
    line_ref[...] = result
    rows = jnp.concatenate([result[:, 128 * h : 128 * (h + 1)] for h in range(4)], axis=0)
    for o in range(32):
        out_ref[20 * o + 16 : 20 * o + 20, :] = rows

    acc[...] = apply() + low[...]

    def step(_, c):
        acc[...] = apply()
        return c

    lax.fori_loop(0, 2 * q + 1, step, 0)
    for o in range(32):
        z, y = divmod(o, 8)
        out_ref[20 * o : 20 * o + 16, :] = acc[16 * y : 16 * y + 16, 128 * z : 128 * (z + 1)]


def exchange(v, axes):
    return lax.all_to_all(v, axes, split_axis=0, concat_axis=0, tiled=True)


def shards(
    fluid_adjoint,
    fluid_source,
    inverse_x,
    inverse_y,
    inverse_z,
    face_cells,
    face_weight,
    face_owner,
    face_solid,
    solid_inverse,
    solid_source,
):
    shape = jax.ShapeDtypeStruct
    group = ("gz", "gy")
    block = shape((128, 128), F32)
    block_vmem = pltpu.VMEM((128, 128), F32)
    dma = pltpu.SemaphoreType.DMA
    packed, table = call(
        pack_body,
        (shape((16 * 17, 128), F32), block),
        fluid_adjoint.reshape(128, 128),
        fluid_source.reshape(128, 128),
        inverse_x,
        specs=[ANY] * 3,
        scratch=[block_vmem, pltpu.VMEM((8, 8), F32), dma((3,))],
        limit=None,
    )
    lines = exchange(packed.reshape(16, 17, 1, 128), "gx").reshape(16 * 17, 128)

    face_args = (face_cells.T, face_weight.T, face_owner.reshape(1, 512), face_solid.reshape(1, 512))
    terms, token = call(
        lines_body,
        (shape((896, 128), F32), shape((8, 128), F32)),
        lines,
        scratch=[pltpu.VMEM((128, 256 * (SWEEPS + 1)), F32)],
    )
    back = exchange(terms.reshape(16, 56, 128), "gx").reshape(896, 128)

    heat, y_rows, inv_z, low, high = call(
        send_body,
        (block, shape((8, 128), F32), block, shape((32, 128), F32), shape((32, 128), F32)),
        table,
        *face_args,
        inverse_y,
        inverse_z,
        token,
    )
    others = [lax.ppermute(inv_z, "gz", [(i, i ^ d) for i in range(4)]) for d in (1, 2, 3)]
    op_z = call(
        prepare_body,
        shape((2, 512, 512), BF16),
        inv_z,
        *others,
        scratch=[pltpu.VMEM((4, 128, 128), F32)],
    )
    inverse = call(
        split_body,
        shape((2, 512, 512), BF16),
        solid_inverse,
        token,
        specs=[ANY] * 2,
        scratch=[pltpu.VMEM((512, 512), F32), dma((1,))],
    )

    up = [(i, i + 1) for i in range(15)]
    near = call(
        near_body,
        block,
        table,
        lax.ppermute(high, "gx", up),
        lax.ppermute(low, "gx", [(j, i) for i, j in up]),
        fluid_source.reshape(128, 128),
        inverse_x,
        specs=[VM] * 3 + [ANY, pl.BlockSpec(memory_space=pltpu.SMEM)],
        scratch=[block_vmem, dma((1,))],
    )

    dealt, first = call(
        deal_body,
        (shape((1280, 128), F32), block),
        back,
        table,
        near,
        heat,
        y_rows,
        op_z,
        inverse,
        specs=[VM] * 5 + [ANY] * 2,
    )
    planes = exchange(dealt.reshape(32, 40, 128), group)
    swept, solid_line = call(
        planes_body,
        (shape((640, 128), F32), shape((1, 512), F32)),
        planes,
        op_z,
        solid_source.reshape(4, 128),
        inverse,
        scratch=[pltpu.VMEM((128, 512), F32), pltpu.VMEM((128, 512), F32), block_vmem],
    )
    parts = exchange(swept.reshape(32, 20, 1, 128), group).reshape(640, 128)
    result = call(finish_body, shape((8, 16, 128), F32), parts, first, *face_args, scratch=[block_vmem])
    return result, solid_line.reshape(512)


def solution(mesh):
    in_specs = (
        P("gx", "gy", "gz"),
        P("gx", "gy", "gz"),
        P("gx", None),
        P("gy", None),
        P("gz", None),
        P(("gx", "gy", "gz"), None),
        P(("gx", "gy", "gz"), None),
        P(("gx", "gy", "gz"), None),
        P(("gx", "gy", "gz")),
        P(("gx", "gy", "gz"), None),
        P(("gx", "gy", "gz")),
    )
    out_specs = (P("gx", "gy", "gz"), P(("gx", "gy", "gz")))
    return jax.shard_map(shards, mesh=mesh, in_specs=in_specs, out_specs=out_specs, check_vma=False)
```

```python
import math
import jax
import jax.numpy as jnp
from jax import lax
from jax.experimental import pallas as pl
from jax.experimental.pallas import tpu as pltpu
from jax.sharding import PartitionSpec as P

SWEEPS = 8
RELAX = 0.15
SPREAD = 0.06
COUPLE = 0.5
SHIFT = 0.25

F32 = jnp.float32
BF16 = jnp.bfloat16
VMEM_LIMIT = 16 * 1024 * 1024
HI = lax.Precision.HIGHEST


def iota(shape, dim):
    return lax.broadcasted_iota(jnp.int32, shape, dim)


def dot(a, b, dims=((1,), (0,)), precision=HI):
    return lax.dot_general(a, b, (dims, ((), ())), precision=precision, preferred_element_type=F32)


def narrow_dot(a, b, dims=((1,), (0,))):
    return lax.dot_general(a, b, (dims, ((), ())), preferred_element_type=F32)


def split2(v):
    p1 = v.astype(BF16)
    return p1, (v - p1.astype(F32)).astype(BF16)


def split3(v):
    p1 = v.astype(BF16)
    rest = v - p1.astype(F32)
    p2 = rest.astype(BF16)
    p3 = (rest - p2.astype(F32)).astype(BF16)
    return p1, p2, p3


def hot_dot(values, hot, dims):
    parts = [narrow_dot(p, hot, dims) for p in split3(values)]
    return parts[0] + (parts[1] + parts[2])


def hot_rows(index_row, count):
    return iota((count, index_row.shape[1]), 0) == index_row


def ones_of(mask):
    return jnp.where(mask, 1.0, 0.0).astype(BF16)


def weights_of(far):
    return jnp.where(
        far == 0, -30.0 / 12.0, jnp.where(far == 1, 16.0 / 12.0, jnp.where(far == 2, -1.0 / 12.0, 0.0))
    )


VM = pl.BlockSpec(memory_space=pltpu.VMEM)
ANY = pl.BlockSpec(memory_space=pl.ANY)


def call(body, outs, *args, specs=None, scratch=(), limit=VMEM_LIMIT, flops=1000000, touched=100000):
    return pl.pallas_call(
        body,
        out_shape=outs,
        in_specs=[VM] * len(args) if specs is None else specs,
        out_specs=jax.tree.map(lambda _: VM, outs),
        scratch_shapes=list(scratch),
        compiler_params=pltpu.CompilerParams(vmem_limit_bytes=limit),
        cost_estimate=pl.CostEstimate(flops=flops, bytes_accessed=touched, transcendentals=0),
    )(*args)


def load_all(sem, pairs):
    copies = [pltpu.make_async_copy(src, dst, sem.at[n]) for n, (src, dst) in enumerate(pairs)]
    for c in copies:
        c.start()
    for c in copies:
        c.wait()


def stack_left(a):
    high, low = split2(a)
    zero = jnp.zeros(low.shape, BF16)
    return jnp.concatenate(
        [jnp.concatenate([high, high], axis=1), jnp.concatenate([low, zero], axis=1)], axis=0
    )


def wide_dot(left, b):
    high, low = split2(b)
    both = narrow_dot(left, jnp.concatenate([high, low], axis=0))
    return both[0:128] + both[128:256]


def put_split(ref, cols, value):
    high, low = split2(value)
    ref[0, :, cols] = high
    ref[1, :, cols] = low


def pack_body(table_hbm, source_hbm, inv_hbm, out_ref, table_ref, source_ref, inv_ref, sem):
    load_all(sem, [(table_hbm, table_ref), (source_hbm, source_ref), (inv_hbm, inv_ref)])
    inv = jnp.concatenate([inv_ref[r : r + 1, :] for r in range(8)] + [jnp.zeros((1, 64), F32)], axis=1)
    for y in range(16):
        out_ref[17 * y : 17 * y + 8, :] = table_ref[pl.ds(y, 8, stride=16), :]
        out_ref[17 * y + 8 : 17 * y + 16, :] = source_ref[pl.ds(y, 8, stride=16), :]
        out_ref[17 * y + 16 : 17 * y + 17, :] = inv


def lines_body(recv_ref, out_ref, token_ref, power):
    token_ref[...] = jnp.zeros((8, 128), F32)
    row, col = iota((128, 128), 0), iota((128, 128), 1)
    inv = recv_ref[pl.ds(16, 16, stride=17), :]
    rows = jnp.where((iota((128, 16), 0) >> 3) == iota((128, 16), 1), 1.0, 0.0).astype(BF16)
    first, second = split2(inv)
    wide = narrow_dot(rows, first) + narrow_dot(rows, second)
    wide = jnp.where((row & 7) == (col & 7), wide, 0.0)
    pick = ones_of((row < 64) & ((row >> 3) == (col & 7)))
    first, second = split2(wide)
    diag = narrow_dot(first, pick) + narrow_dot(second, pick)
    diag = jnp.where((row >> 3) == (col >> 3), diag, 0.0)
    far = jnp.abs(row - col)
    first, second = split2(diag)
    band = jnp.where(far == 0, -30.0, jnp.where(far == 1, 16.0, jnp.where(far == 2, -1.0, 0.0))).astype(BF16)
    op = (SPREAD / 12.0) * (narrow_dot(first, band) + narrow_dot(second, band)) + jnp.where(far == 0, SHIFT, 0.0)
    for f in range(2):
        power[:, 128 * f : 128 * f + 128] = jnp.concatenate(
            [recv_ref[17 * g + 8 * f : 17 * g + 8 * f + 8, :] for g in range(16)], axis=0
        )

    def store(k, value):
        power[:, 256 * k : 256 * k + value.shape[1]] = value

    both = wide_dot(stack_left(op), jnp.concatenate([op, power[:, 0:256]], axis=1))
    store(1, both[:, 128:])
    both = wide_dot(stack_left(both[:, 0:128]), jnp.concatenate([both[:, 0:128], power[:, 0:512]], axis=1))
    store(2, both[:, 128:])
    four = stack_left(both[:, 0:128])
    store(4, wide_dot(four, power[:, 0:1024]))
    store(8, wide_dot(four, power[:, 1024 : 1024 + 128]))
    for m in range(SWEEPS - 1):
        total = float(math.comb(SWEEPS, m)) * power[:, 256 * (SWEEPS - m) : 256 * (SWEEPS - m) + 128]
        for i in range(m, SWEEPS):
            total = total + RELAX * math.comb(i, m) * power[:, 256 * (i - m) + 128 : 256 * (i - m) + 256]
        for g in range(16):
            out_ref[56 * g + 8 * m : 56 * g + 8 * m + 8, :] = total[8 * g : 8 * g + 8]


def near_body(table_ref, low_ref, high_ref, source_hbm, inv_ref, out_ref, source_ref, sem):
    load_all(sem, [(source_hbm, source_ref)])
    layers = [low_ref[0:16, :], low_ref[16:32, :]]
    layers += [table_ref[16 * x : 16 * x + 16, :] for x in range(8)]
    layers += [high_ref[0:16, :], high_ref[16:32, :]]
    sums = [
        16.0 * (layers[x + 1] + layers[x + 3]) - 30.0 * layers[x + 2] - layers[x] - layers[x + 4] for x in range(8)
    ]
    for i in range(8):
        total = sums[0] * inv_ref[0, i]
        for r in range(1, 8):
            total = total + sums[r] * inv_ref[r, i]
        total = (SPREAD / 12.0) * total + SHIFT * layers[i + 2]
        rows = slice(16 * i, 16 * i + 16)
        out_ref[rows, :] = SWEEPS * total + RELAX * source_ref[rows, :]


def deal_body(recv_ref, table_ref, near_ref, heat_ref, rows_ref, after_one, after_two, out_ref, first_ref):
    for m in range(SWEEPS - 1):
        for y in range(16):
            rows = recv_ref[56 * y + 8 * m : 56 * y + 8 * m + 8, :]
            if m == 0:
                first_ref[pl.ds(y, 8, stride=16), :] = rows
            else:
                q, half = divmod(m - 1, 2)
                out_ref[pl.ds(40 * q + 16 * half + y, 8, stride=160), :] = rows
    for x in range(8):
        out_ref[160 * x + 120 : 160 * x + 136, :] = near_ref[16 * x : 16 * x + 16, :]
        out_ref[160 * x + 136 : 160 * x + 152, :] = table_ref[16 * x : 16 * x + 16, :]
    for h in range(4):
        out_ref[pl.ds(32 + h, 32, stride=40), :] = heat_ref[h * 32 : (h + 1) * 32, :]
    for o in range(32):
        out_ref[40 * o + 36 : 40 * o + 40, :] = rows_ref[0:4, :]


def send_body(table_ref, cells_ref, weight_ref, owner_ref, solid_ref, inv_y_ref, inv_z_in, after_ref, out_ref, rows_ref, inv_z_ref, low_ref, high_ref):
    gy = lax.axis_index("gy")
    gz = lax.axis_index("gz")
    inv_z_ref[...] = inv_z_in[...]
    low_ref[...] = table_ref[0:32, :]
    high_ref[...] = table_ref[96:128, :]
    table = table_ref[...]
    acc = None
    for k in range(4):
        cell = cells_ref[k : k + 1, :]
        hot = ones_of(hot_rows(cell >> 7, 128))
        spread = jnp.where(hot_rows(cell & 127, 128), weight_ref[k : k + 1, :], 0.0)
        term = hot_dot(table, hot, ((0,), (0,))) * spread
        acc = term if acc is None else acc + term
    flux = jnp.sum(acc, axis=0, keepdims=True)
    solid = solid_ref[...]
    owner = owner_ref[...]
    rank = (owner & 3) * 8 + (owner >> 2)
    hot_hi = ones_of(hot_rows((solid >> 7) * 32 + rank, 128))
    out_ref[...] = hot_dot(jnp.where(hot_rows(solid & 127, 128), flux, 0.0), hot_hi, ((1,), (1,))).T
    shift = iota((16, 128), 1) - gy * 16 - iota((16, 128), 0)
    own = SPREAD * dot(inv_y_ref[...], weights_of(jnp.abs(shift)), ((0,), (0,)))
    own = own + jnp.where(shift == 0, 1.0 - RELAX - SHIFT, 0.0)
    pick = jnp.where(iota((8, 16), 1) == iota((8, 16), 0) + gz * 4, 1.0, 0.0)
    rows_ref[...] = dot(pick, own)


def split_body(value_hbm, after_hbm, out_ref, value_ref, sem):
    load_all(sem, [(value_hbm, value_ref)])
    put_split(out_ref, slice(0, 512), value_ref[...])


def finish_body(recv_ref, first_ref, cells_ref, weight_ref, owner_ref, solid_ref, out_ref, stage):
    for o in range(32):
        owner = (o % 8) * 4 + o // 8
        stage[4 * owner : 4 * owner + 4, :] = recv_ref[20 * o + 16 : 20 * o + 20, :]
    solid = solid_ref[...]
    hot = ones_of(hot_rows(owner_ref[...] * 4 + (solid >> 7), 128))
    high, rest = split2(stage[...])
    picked = narrow_dot(high, hot, ((0,), (0,))) + narrow_dot(rest, hot, ((0,), (0,)))
    temp = COUPLE * jnp.sum(jnp.where(hot_rows(solid & 127, 128), picked, 0.0), axis=0, keepdims=True)
    hots, highs, rests = [], [], []
    for k in range(4):
        cell = cells_ref[k : k + 1, :]
        hots.append(ones_of(hot_rows(cell >> 7, 128)))
        high, rest = split2(jnp.where(hot_rows(cell & 127, 128), temp * weight_ref[k : k + 1, :], 0.0))
        highs.append(high)
        rests.append(rest)
    hot = jnp.concatenate(hots, axis=1)
    values = jnp.concatenate([jnp.concatenate(highs, axis=1), jnp.concatenate(rests, axis=1)], axis=0)
    both = narrow_dot(hot, values, ((1,), (1,)))
    total = both[:, 0:128] + both[:, 128:256]
    for i in range(8):
        parts = [recv_ref[20 * o : 20 * o + 16, :] for o in range(4 * i, 4 * i + 4)]
        part = (parts[0] + parts[1]) + (parts[2] + parts[3])
        rows = slice(16 * i, 16 * i + 16)
        out_ref[i] = part + first_ref[rows, :] + total[rows, :]


def prepare_body(own_ref, one_ref, two_ref, three_ref, op_z_ref, mats):
    gz = lax.axis_index("gz")
    for d, ref in enumerate((own_ref, one_ref, two_ref, three_ref)):
        mats[jnp.bitwise_xor(gz, d)] = ref[...]
    for k in range(4):
        far = jnp.abs(iota((512, 128), 0) - (iota((512, 128), 1) + 128 * k))
        put_split(op_z_ref, slice(128 * k, 128 * k + 128), SPREAD * dot(weights_of(far), mats[k]))


def planes_body(recv_ref, op_z_ref, source_ref, inverse_ref, out_ref, line_ref, low, acc, op_y):
    q = lax.rem(lax.axis_index("gy"), 4)
    for o in range(32):
        z, y = divmod(o, 8)
        low[16 * y : 16 * y + 16, 128 * z : 128 * (z + 1)] = recv_ref[o, 0:16]
        acc[16 * y : 16 * y + 16, 128 * z : 128 * (z + 1)] = recv_ref[o, 16:32]
        op_y[16 * y + 4 * z : 16 * y + 4 * z + 4, :] = recv_ref[o, 36:40]
    y_left = stack_left(op_y[...])

    right = op_z_ref[0, 240:256, 256:384].astype(F32) + op_z_ref[1, 240:256, 256:384].astype(F32)
    left = op_z_ref[0, 256:272, 128:256].astype(F32) + op_z_ref[1, 256:272, 128:256].astype(F32)

    def apply():
        v = acc[...]
        high, rest = split2(v)
        both = jnp.concatenate([high, rest], axis=0)
        y = narrow_dot(y_left, both)
        y = y[0:128] + y[128:256]
        halves = []
        for n in range(2):
            part = slice(256 * n, 256 * n + 256)
            z = narrow_dot(both[:, part], op_z_ref[0, part, part])
            halves.append(y[:, part] + (z[0:128] + z[128:256]) + narrow_dot(high[:, part], op_z_ref[1, part, part]))
        to_right = v[:, 254:255] * right[14:15] + v[:, 255:256] * right[15:16]
        to_left = v[:, 256:257] * left[0:1] + v[:, 257:258] * left[1:2]
        return jnp.concatenate(
            [halves[0][:, 0:128], halves[0][:, 128:256] + to_left, halves[1][:, 0:128] + to_right, halves[1][:, 128:256]],
            axis=1,
        )

    heat = jnp.sum(recv_ref[:, 32:40, :], axis=0)[0:4, :] + source_ref[...]
    high, rest = split2(jnp.concatenate([heat[h : h + 1, :] for h in range(4)], axis=1))
    both = jnp.concatenate([high.astype(F32), rest.astype(F32), jnp.zeros((6, 512), F32)], axis=0).astype(BF16)
    result = narrow_dot(both, inverse_ref[0])
    result = (result[0:1] + result[1:2]) + narrow_dot(both, inverse_ref[1])[0:1]
    line_ref[...] = result
    rows = jnp.concatenate([result[:, 128 * h : 128 * (h + 1)] for h in range(4)], axis=0)
    for o in range(32):
        out_ref[20 * o + 16 : 20 * o + 20, :] = rows

    acc[...] = apply() + low[...]

    def step(_, c):
        acc[...] = apply()
        return c

    lax.fori_loop(0, 2 * q + 1, step, 0)
    for o in range(32):
        z, y = divmod(o, 8)
        out_ref[20 * o : 20 * o + 16, :] = acc[16 * y : 16 * y + 16, 128 * z : 128 * (z + 1)]


def exchange(v, axes):
    return lax.all_to_all(v, axes, split_axis=0, concat_axis=0, tiled=True)


def shards(
    fluid_adjoint,
    fluid_source,
    inverse_x,
    inverse_y,
    inverse_z,
    face_cells,
    face_weight,
    face_owner,
    face_solid,
    solid_inverse,
    solid_source,
):
    shape = jax.ShapeDtypeStruct
    group = ("gz", "gy")
    block = shape((128, 128), F32)
    block_vmem = pltpu.VMEM((128, 128), F32)
    dma = pltpu.SemaphoreType.DMA
    packed, table = call(
        pack_body,
        (shape((16 * 17, 128), F32), block),
        fluid_adjoint.reshape(128, 128),
        fluid_source.reshape(128, 128),
        inverse_x,
        specs=[ANY] * 3,
        scratch=[block_vmem, pltpu.VMEM((8, 8), F32), dma((3,))],
        limit=None,
    )
    lines = exchange(packed.reshape(16, 17, 1, 128), "gx").reshape(16 * 17, 128)

    face_args = (face_cells.T, face_weight.T, face_owner.reshape(1, 512), face_solid.reshape(1, 512))
    terms, token = call(
        lines_body,
        (shape((896, 128), F32), shape((8, 128), F32)),
        lines,
        scratch=[pltpu.VMEM((128, 256 * (SWEEPS + 1)), F32)],
    )
    back = exchange(terms.reshape(16, 56, 128), "gx").reshape(896, 128)

    heat, y_rows, inv_z, low, high = call(
        send_body,
        (block, shape((8, 128), F32), block, shape((32, 128), F32), shape((32, 128), F32)),
        table,
        *face_args,
        inverse_y,
        inverse_z,
        token,
    )
    others = [lax.ppermute(inv_z, "gz", [(i, i ^ d) for i in range(4)]) for d in (1, 2, 3)]
    op_z = call(
        prepare_body,
        shape((2, 512, 512), BF16),
        inv_z,
        *others,
        scratch=[pltpu.VMEM((4, 128, 128), F32)],
    )
    inverse = call(
        split_body,
        shape((2, 512, 512), BF16),
        solid_inverse,
        token,
        specs=[ANY] * 2,
        scratch=[pltpu.VMEM((512, 512), F32), dma((1,))],
    )

    up = [(i, i + 1) for i in range(15)]
    near = call(
        near_body,
        block,
        table,
        lax.ppermute(high, "gx", up),
        lax.ppermute(low, "gx", [(j, i) for i, j in up]),
        fluid_source.reshape(128, 128),
        inverse_x,
        specs=[VM] * 3 + [ANY, pl.BlockSpec(memory_space=pltpu.SMEM)],
        scratch=[block_vmem, dma((1,))],
    )

    dealt, first = call(
        deal_body,
        (shape((1280, 128), F32), block),
        back,
        table,
        near,
        heat,
        y_rows,
        op_z,
        inverse,
        specs=[VM] * 5 + [ANY] * 2,
    )
    planes = exchange(dealt.reshape(32, 40, 128), group)
    swept, solid_line = call(
        planes_body,
        (shape((640, 128), F32), shape((1, 512), F32)),
        planes,
        op_z,
        solid_source.reshape(4, 128),
        inverse,
        scratch=[pltpu.VMEM((128, 512), F32), pltpu.VMEM((128, 512), F32), block_vmem],
    )
    parts = exchange(swept.reshape(32, 20, 1, 128), group).reshape(640, 128)
    result = call(finish_body, shape((8, 16, 128), F32), parts, first, *face_args, scratch=[block_vmem])
    return result, solid_line.reshape(512)


def solution(mesh):
    in_specs = (
        P("gx", "gy", "gz"),
        P("gx", "gy", "gz"),
        P("gx", None),
        P("gy", None),
        P("gz", None),
        P(("gx", "gy", "gz"), None),
        P(("gx", "gy", "gz"), None),
        P(("gx", "gy", "gz"), None),
        P(("gx", "gy", "gz")),
        P(("gx", "gy", "gz"), None),
        P(("gx", "gy", "gz")),
    )
    out_specs = (P("gx", "gy", "gz"), P(("gx", "gy", "gz")))
    return jax.shard_map(shards, mesh=mesh, in_specs=in_specs, out_specs=out_specs, check_vma=False)
```

```python
import math
import jax
import jax.numpy as jnp
from jax import lax
from jax.experimental import pallas as pl
from jax.experimental.pallas import tpu as pltpu
from jax.sharding import PartitionSpec as P

SWEEPS = 8
RELAX = 0.15
SPREAD = 0.06
COUPLE = 0.5
SHIFT = 0.25

F32 = jnp.float32
BF16 = jnp.bfloat16
VMEM_LIMIT = 16 * 1024 * 1024
HI = lax.Precision.HIGHEST


def iota(shape, dim):
    return lax.broadcasted_iota(jnp.int32, shape, dim)


def dot(a, b, dims=((1,), (0,)), precision=HI):
    return lax.dot_general(a, b, (dims, ((), ())), precision=precision, preferred_element_type=F32)


def narrow_dot(a, b, dims=((1,), (0,))):
    return lax.dot_general(a, b, (dims, ((), ())), preferred_element_type=F32)


def split2(v):
    p1 = v.astype(BF16)
    return p1, (v - p1.astype(F32)).astype(BF16)


def split3(v):
    p1 = v.astype(BF16)
    rest = v - p1.astype(F32)
    p2 = rest.astype(BF16)
    p3 = (rest - p2.astype(F32)).astype(BF16)
    return p1, p2, p3


def hot_dot(values, hot, dims):
    parts = [narrow_dot(p, hot, dims) for p in split3(values)]
    return parts[0] + (parts[1] + parts[2])


def hot_rows(index_row, count):
    return iota((count, index_row.shape[1]), 0) == index_row


def ones_of(mask):
    return jnp.where(mask, 1.0, 0.0).astype(BF16)


def weights_of(far):
    return jnp.where(
        far == 0, -30.0 / 12.0, jnp.where(far == 1, 16.0 / 12.0, jnp.where(far == 2, -1.0 / 12.0, 0.0))
    )


VM = pl.BlockSpec(memory_space=pltpu.VMEM)
ANY = pl.BlockSpec(memory_space=pl.ANY)


def call(body, outs, *args, specs=None, scratch=(), limit=VMEM_LIMIT, flops=1000000, touched=100000):
    return pl.pallas_call(
        body,
        out_shape=outs,
        in_specs=[VM] * len(args) if specs is None else specs,
        out_specs=jax.tree.map(lambda _: VM, outs),
        scratch_shapes=list(scratch),
        compiler_params=pltpu.CompilerParams(vmem_limit_bytes=limit),
        cost_estimate=pl.CostEstimate(flops=flops, bytes_accessed=touched, transcendentals=0),
    )(*args)


def load_all(sem, pairs):
    copies = [pltpu.make_async_copy(src, dst, sem.at[n]) for n, (src, dst) in enumerate(pairs)]
    for c in copies:
        c.start()
    for c in copies:
        c.wait()


def stack_left(a):
    high, low = split2(a)
    zero = jnp.zeros(low.shape, BF16)
    return jnp.concatenate(
        [jnp.concatenate([high, high], axis=1), jnp.concatenate([low, zero], axis=1)], axis=0
    )


def wide_dot(left, b):
    high, low = split2(b)
    both = narrow_dot(left, jnp.concatenate([high, low], axis=0))
    return both[0:128] + both[128:256]


def put_split(ref, cols, value):
    high, low = split2(value)
    ref[0, :, cols] = high
    ref[1, :, cols] = low


def pack_body(table_hbm, source_hbm, inv_hbm, out_ref, table_ref, source_ref, inv_ref, sem):
    load_all(sem, [(table_hbm, table_ref), (source_hbm, source_ref), (inv_hbm, inv_ref)])
    inv = jnp.concatenate([inv_ref[r : r + 1, :] for r in range(8)] + [jnp.zeros((1, 64), F32)], axis=1)
    for y in range(16):
        out_ref[17 * y : 17 * y + 8, :] = table_ref[pl.ds(y, 8, stride=16), :]
        out_ref[17 * y + 8 : 17 * y + 16, :] = source_ref[pl.ds(y, 8, stride=16), :]
        out_ref[17 * y + 16 : 17 * y + 17, :] = inv


def lines_body(recv_ref, out_ref, token_ref, power):
    token_ref[...] = jnp.zeros((8, 128), F32)
    row, col = iota((128, 128), 0), iota((128, 128), 1)
    inv = recv_ref[pl.ds(16, 16, stride=17), :]
    rows = jnp.where((iota((128, 16), 0) >> 3) == iota((128, 16), 1), 1.0, 0.0).astype(BF16)
    first, second = split2(inv)
    wide = narrow_dot(rows, first) + narrow_dot(rows, second)
    wide = jnp.where((row & 7) == (col & 7), wide, 0.0)
    pick = ones_of((row < 64) & ((row >> 3) == (col & 7)))
    first, second = split2(wide)
    diag = narrow_dot(first, pick) + narrow_dot(second, pick)
    diag = jnp.where((row >> 3) == (col >> 3), diag, 0.0)
    far = jnp.abs(row - col)
    first, second = split2(diag)
    band = jnp.where(far == 0, -30.0, jnp.where(far == 1, 16.0, jnp.where(far == 2, -1.0, 0.0))).astype(BF16)
    op = (SPREAD / 12.0) * (narrow_dot(first, band) + narrow_dot(second, band)) + jnp.where(far == 0, SHIFT, 0.0)
    for f in range(2):
        power[:, 128 * f : 128 * f + 128] = jnp.concatenate(
            [recv_ref[17 * g + 8 * f : 17 * g + 8 * f + 8, :] for g in range(16)], axis=0
        )

    def store(k, value):
        power[:, 256 * k : 256 * k + value.shape[1]] = value

    both = wide_dot(stack_left(op), jnp.concatenate([op, power[:, 0:256]], axis=1))
    store(1, both[:, 128:])
    both = wide_dot(stack_left(both[:, 0:128]), jnp.concatenate([both[:, 0:128], power[:, 0:512]], axis=1))
    store(2, both[:, 128:])
    four = stack_left(both[:, 0:128])
    store(4, wide_dot(four, power[:, 0:1024]))
    store(8, wide_dot(four, power[:, 1024 : 1024 + 128]))
    for m in range(SWEEPS - 1):
        total = float(math.comb(SWEEPS, m)) * power[:, 256 * (SWEEPS - m) : 256 * (SWEEPS - m) + 128]
        for i in range(m, SWEEPS):
            total = total + RELAX * math.comb(i, m) * power[:, 256 * (i - m) + 128 : 256 * (i - m) + 256]
        for g in range(16):
            out_ref[56 * g + 8 * m : 56 * g + 8 * m + 8, :] = total[8 * g : 8 * g + 8]


def near_body(table_ref, low_ref, high_ref, source_hbm, inv_ref, out_ref, source_ref, sem):
    load_all(sem, [(source_hbm, source_ref)])
    layers = [low_ref[0:16, :], low_ref[16:32, :]]
    layers += [table_ref[16 * x : 16 * x + 16, :] for x in range(8)]
    layers += [high_ref[0:16, :], high_ref[16:32, :]]
    sums = [
        16.0 * (layers[x + 1] + layers[x + 3]) - 30.0 * layers[x + 2] - layers[x] - layers[x + 4] for x in range(8)
    ]
    for i in range(8):
        total = sums[0] * inv_ref[0, i]
        for r in range(1, 8):
            total = total + sums[r] * inv_ref[r, i]
        total = (SPREAD / 12.0) * total + SHIFT * layers[i + 2]
        rows = slice(16 * i, 16 * i + 16)
        out_ref[rows, :] = SWEEPS * total + RELAX * source_ref[rows, :]


def deal_body(recv_ref, table_ref, near_ref, heat_ref, rows_ref, after_one, after_two, out_ref, first_ref):
    for m in range(SWEEPS - 1):
        for y in range(16):
            rows = recv_ref[56 * y + 8 * m : 56 * y + 8 * m + 8, :]
            if m == 0:
                first_ref[pl.ds(y, 8, stride=16), :] = rows
            else:
                q, half = divmod(m - 1, 2)
                out_ref[pl.ds(40 * q + 16 * half + y, 8, stride=160), :] = rows
    for x in range(8):
        out_ref[160 * x + 120 : 160 * x + 136, :] = near_ref[16 * x : 16 * x + 16, :]
        out_ref[160 * x + 136 : 160 * x + 152, :] = table_ref[16 * x : 16 * x + 16, :]
    for h in range(4):
        out_ref[pl.ds(32 + h, 32, stride=40), :] = heat_ref[h * 32 : (h + 1) * 32, :]
    for o in range(32):
        out_ref[40 * o + 36 : 40 * o + 40, :] = rows_ref[0:4, :]


def send_body(table_ref, cells_ref, weight_ref, owner_ref, solid_ref, inv_y_ref, inv_z_in, after_ref, out_ref, rows_ref, inv_z_ref, low_ref, high_ref):
    gy = lax.axis_index("gy")
    gz = lax.axis_index("gz")
    inv_z_ref[...] = inv_z_in[...]
    low_ref[...] = table_ref[0:32, :]
    high_ref[...] = table_ref[96:128, :]
    table = table_ref[...]
    acc = None
    for k in range(4):
        cell = cells_ref[k : k + 1, :]
        hot = ones_of(hot_rows(cell >> 7, 128))
        spread = jnp.where(hot_rows(cell & 127, 128), weight_ref[k : k + 1, :], 0.0)
        term = hot_dot(table, hot, ((0,), (0,))) * spread
        acc = term if acc is None else acc + term
    flux = jnp.sum(acc, axis=0, keepdims=True)
    solid = solid_ref[...]
    owner = owner_ref[...]
    rank = (owner & 3) * 8 + (owner >> 2)
    hot_hi = ones_of(hot_rows((solid >> 7) * 32 + rank, 128))
    out_ref[...] = hot_dot(jnp.where(hot_rows(solid & 127, 128), flux, 0.0), hot_hi, ((1,), (1,))).T
    shift = iota((16, 128), 1) - gy * 16 - iota((16, 128), 0)
    own = SPREAD * dot(inv_y_ref[...], weights_of(jnp.abs(shift)), ((0,), (0,)))
    own = own + jnp.where(shift == 0, 1.0 - RELAX - SHIFT, 0.0)
    pick = jnp.where(iota((8, 16), 1) == iota((8, 16), 0) + gz * 4, 1.0, 0.0)
    rows_ref[...] = dot(pick, own)


def split_body(value_hbm, after_hbm, out_ref, value_ref, sem):
    load_all(sem, [(value_hbm, value_ref)])
    put_split(out_ref, slice(0, 512), value_ref[...])


def finish_body(recv_ref, first_ref, cells_ref, weight_ref, owner_ref, solid_ref, out_ref, stage):
    for o in range(32):
        owner = (o % 8) * 4 + o // 8
        stage[4 * owner : 4 * owner + 4, :] = recv_ref[20 * o + 16 : 20 * o + 20, :]
    solid = solid_ref[...]
    hot = ones_of(hot_rows(owner_ref[...] * 4 + (solid >> 7), 128))
    high, rest = split2(stage[...])
    picked = narrow_dot(high, hot, ((0,), (0,))) + narrow_dot(rest, hot, ((0,), (0,)))
    temp = COUPLE * jnp.sum(jnp.where(hot_rows(solid & 127, 128), picked, 0.0), axis=0, keepdims=True)
    hots, highs, rests = [], [], []
    for k in range(4):
        cell = cells_ref[k : k + 1, :]
        hots.append(ones_of(hot_rows(cell >> 7, 128)))
        high, rest = split2(jnp.where(hot_rows(cell & 127, 128), temp * weight_ref[k : k + 1, :], 0.0))
        highs.append(high)
        rests.append(rest)
    hot = jnp.concatenate(hots, axis=1)
    values = jnp.concatenate([jnp.concatenate(highs, axis=1), jnp.concatenate(rests, axis=1)], axis=0)
    both = narrow_dot(hot, values, ((1,), (1,)))
    total = both[:, 0:128] + both[:, 128:256]
    for i in range(8):
        parts = [recv_ref[20 * o : 20 * o + 16, :] for o in range(4 * i, 4 * i + 4)]
        part = (parts[0] + parts[1]) + (parts[2] + parts[3])
        rows = slice(16 * i, 16 * i + 16)
        out_ref[i] = part + first_ref[rows, :] + total[rows, :]


def prepare_body(own_ref, one_ref, two_ref, three_ref, op_z_ref, mats):
    gz = lax.axis_index("gz")
    for d, ref in enumerate((own_ref, one_ref, two_ref, three_ref)):
        mats[jnp.bitwise_xor(gz, d)] = ref[...]
    for k in range(4):
        far = jnp.abs(iota((512, 128), 0) - (iota((512, 128), 1) + 128 * k))
        put_split(op_z_ref, slice(128 * k, 128 * k + 128), SPREAD * dot(weights_of(far), mats[k]))


def planes_body(recv_ref, op_z_ref, source_ref, inverse_ref, out_ref, line_ref, low, acc, op_y):
    q = lax.rem(lax.axis_index("gy"), 4)
    for o in range(32):
        z, y = divmod(o, 8)
        low[16 * y : 16 * y + 16, 128 * z : 128 * (z + 1)] = recv_ref[o, 0:16]
        acc[16 * y : 16 * y + 16, 128 * z : 128 * (z + 1)] = recv_ref[o, 16:32]
        op_y[16 * y + 4 * z : 16 * y + 4 * z + 4, :] = recv_ref[o, 36:40]
    y_left = stack_left(op_y[...])

    right = op_z_ref[0, 240:256, 256:384].astype(F32) + op_z_ref[1, 240:256, 256:384].astype(F32)
    left = op_z_ref[0, 256:272, 128:256].astype(F32) + op_z_ref[1, 256:272, 128:256].astype(F32)

    def apply(v):
        high, rest = split2(v)
        both = jnp.concatenate([high, rest], axis=0)
        y = narrow_dot(y_left, both)
        y = y[0:128] + y[128:256]
        halves = []
        for n in range(2):
            part = slice(256 * n, 256 * n + 256)
            z = narrow_dot(both[:, part], op_z_ref[0, part, part])
            halves.append(y[:, part] + (z[0:128] + z[128:256]) + narrow_dot(high[:, part], op_z_ref[1, part, part]))
        to_right = v[:, 254:255] * right[14:15] + v[:, 255:256] * right[15:16]
        to_left = v[:, 256:257] * left[0:1] + v[:, 257:258] * left[1:2]
        return jnp.concatenate(
            [halves[0][:, 0:128], halves[0][:, 128:256] + to_left, halves[1][:, 0:128] + to_right, halves[1][:, 128:256]],
            axis=1,
        )

    heat = jnp.sum(recv_ref[:, 32:40, :], axis=0)[0:4, :] + source_ref[...]
    high, rest = split2(jnp.concatenate([heat[h : h + 1, :] for h in range(4)], axis=1))
    both = jnp.concatenate([high.astype(F32), rest.astype(F32), jnp.zeros((6, 512), F32)], axis=0).astype(BF16)
    result = narrow_dot(both, inverse_ref[0])
    result = (result[0:1] + result[1:2]) + narrow_dot(both, inverse_ref[1])[0:1]
    line_ref[...] = result
    rows = jnp.concatenate([result[:, 128 * h : 128 * (h + 1)] for h in range(4)], axis=0)
    for o in range(32):
        out_ref[20 * o + 16 : 20 * o + 20, :] = rows

    acc[...] = apply(apply(acc[...]) + low[...])
    for pair in range(1, 4):

        @pl.when(q >= pair)
        def _():
            acc[...] = apply(apply(acc[...]))

    for o in range(32):
        z, y = divmod(o, 8)
        out_ref[20 * o : 20 * o + 16, :] = acc[16 * y : 16 * y + 16, 128 * z : 128 * (z + 1)]


def exchange(v, axes):
    return lax.all_to_all(v, axes, split_axis=0, concat_axis=0, tiled=True)


def shards(
    fluid_adjoint,
    fluid_source,
    inverse_x,
    inverse_y,
    inverse_z,
    face_cells,
    face_weight,
    face_owner,
    face_solid,
    solid_inverse,
    solid_source,
):
    shape = jax.ShapeDtypeStruct
    group = ("gz", "gy")
    block = shape((128, 128), F32)
    block_vmem = pltpu.VMEM((128, 128), F32)
    dma = pltpu.SemaphoreType.DMA
    packed, table = call(
        pack_body,
        (shape((16 * 17, 128), F32), block),
        fluid_adjoint.reshape(128, 128),
        fluid_source.reshape(128, 128),
        inverse_x,
        specs=[ANY] * 3,
        scratch=[block_vmem, pltpu.VMEM((8, 8), F32), dma((3,))],
        limit=None,
    )
    lines = exchange(packed.reshape(16, 17, 1, 128), "gx").reshape(16 * 17, 128)

    face_args = (face_cells.T, face_weight.T, face_owner.reshape(1, 512), face_solid.reshape(1, 512))
    terms, token = call(
        lines_body,
        (shape((896, 128), F32), shape((8, 128), F32)),
        lines,
        scratch=[pltpu.VMEM((128, 256 * (SWEEPS + 1)), F32)],
    )
    back = exchange(terms.reshape(16, 56, 128), "gx").reshape(896, 128)

    heat, y_rows, inv_z, low, high = call(
        send_body,
        (block, shape((8, 128), F32), block, shape((32, 128), F32), shape((32, 128), F32)),
        table,
        *face_args,
        inverse_y,
        inverse_z,
        token,
    )
    others = [lax.ppermute(inv_z, "gz", [(i, i ^ d) for i in range(4)]) for d in (1, 2, 3)]
    op_z = call(
        prepare_body,
        shape((2, 512, 512), BF16),
        inv_z,
        *others,
        scratch=[pltpu.VMEM((4, 128, 128), F32)],
    )
    inverse = call(
        split_body,
        shape((2, 512, 512), BF16),
        solid_inverse,
        token,
        specs=[ANY] * 2,
        scratch=[pltpu.VMEM((512, 512), F32), dma((1,))],
    )

    up = [(i, i + 1) for i in range(15)]
    near = call(
        near_body,
        block,
        table,
        lax.ppermute(high, "gx", up),
        lax.ppermute(low, "gx", [(j, i) for i, j in up]),
        fluid_source.reshape(128, 128),
        inverse_x,
        specs=[VM] * 3 + [ANY, pl.BlockSpec(memory_space=pltpu.SMEM)],
        scratch=[block_vmem, dma((1,))],
    )

    dealt, first = call(
        deal_body,
        (shape((1280, 128), F32), block),
        back,
        table,
        near,
        heat,
        y_rows,
        op_z,
        inverse,
        specs=[VM] * 5 + [ANY] * 2,
    )
    planes = exchange(dealt.reshape(32, 40, 128), group)
    swept, solid_line = call(
        planes_body,
        (shape((640, 128), F32), shape((1, 512), F32)),
        planes,
        op_z,
        solid_source.reshape(4, 128),
        inverse,
        scratch=[pltpu.VMEM((128, 512), F32), pltpu.VMEM((128, 512), F32), block_vmem],
    )
    parts = exchange(swept.reshape(32, 20, 1, 128), group).reshape(640, 128)
    result = call(finish_body, shape((8, 16, 128), F32), parts, first, *face_args, scratch=[block_vmem])
    return result, solid_line.reshape(512)


def solution(mesh):
    in_specs = (
        P("gx", "gy", "gz"),
        P("gx", "gy", "gz"),
        P("gx", None),
        P("gy", None),
        P("gz", None),
        P(("gx", "gy", "gz"), None),
        P(("gx", "gy", "gz"), None),
        P(("gx", "gy", "gz"), None),
        P(("gx", "gy", "gz")),
        P(("gx", "gy", "gz"), None),
        P(("gx", "gy", "gz")),
    )
    out_specs = (P("gx", "gy", "gz"), P(("gx", "gy", "gz")))
    return jax.shard_map(shards, mesh=mesh, in_specs=in_specs, out_specs=out_specs, check_vma=False)
```
